32 devices in a mesh: rot: 8 (over z, y), fft: 4 (over x, core).
Axes of the slice: x: 2, y: 2, z: 4, core: 2. Of those that a mesh axis runs over, the one named last changes fastest.
Arguments:
- receptor: bfloat16 [2, 11, 128, 128, 128], P(None, None, 'fft'), may hold values from -6 to 6, as said below
- ligand_grids: bfloat16 [32, 11, 32, 1024], P(None, None, 'fft'), may hold values from -8 to 8
- rot_index: int32 [48], P('rot'), parts along dimension 0, may hold values from 0 to 31
Outputs:
- scores: float32 [48, 128, 128, 128], P('rot', 'fft'), parts along dimension 0
- best: float32 [48], P('rot'), parts along dimension 0
The draws below stay inside these ranges and needn't reach their ends.
There are 8 independent parts, one for each index of `rot`. The reference program is written for one: setup_inputs(seed, part) draws one part's arguments, and reference() takes and returns one part's arrays. A program takes and returns all parts, laid end to end along the dimension named above; an argument that names none is the same for every part. Nothing has to cross between parts.
Inputs may be any that keep to these rules, and one draw needn't show every extreme that they name: The receptor spectra are those of real grids: in every channel the entry at frequency (-kz, -kx, -ky), taken modulo 128 along each dimension, is the complex conjugate of the entry at (kz, kx, ky).
All inputs are finite; a program needn't handle non-finite values.
Results may differ from the reference program's by a relative error of at most 0.0003.
Values may be sent and summed in bfloat16 or wider, within the bound.
A program may use at most 256 MiB of HBM per device.

```python
import jax
import jax.numpy as jnp
from jax import lax

N = 128
CH = 11
LB = 32
ROT_SET = 32
ROTS = 6


def draw_receptor(key, part):
    first_key = jax.random.fold_in(key, 0)
    grid_shape = (2, CH, N, N, N)
    sample = jnp.clip(jax.random.normal(first_key, grid_shape, jnp.float32), -4.0, 4.0)
    mirror = jnp.roll(jnp.flip(sample, axis=(2, 3, 4)), 1, axis=(2, 3, 4))
    real_part = (sample[0] + mirror[0]) * 0.5 ** 0.5
    imag_part = (sample[1] - mirror[1]) * 0.5 ** 0.5
    return jnp.stack([real_part, imag_part]).astype(jnp.bfloat16)


def plant(array, own_key, least, largest):
    longest = array.shape.index(max(array.shape))
    spots = []
    for shift in (0, 1):
        where = [jax.random.randint(jax.random.fold_in(own_key, axis), (), 0, length) for axis, length in enumerate(array.shape)]
        where[longest] = (where[longest] + shift) % array.shape[longest]
        spots.append(tuple(where))
    return array.at[spots[0]].set(least).at[spots[1]].set(largest)


def block_levels(key, dims, cuts, least, top_value):
    def one(dim, shards_of):
        heights = jax.random.uniform(jax.random.fold_in(jax.random.fold_in(key, 6), dim), (shards_of,), jnp.float32, least / len(cuts), top_value / len(cuts))
        return jnp.repeat(jnp.exp(heights), dims[dim] // shards_of).reshape((-1,) + (1,) * (len(dims) - dim - 1))

    loudness = one(*cuts[0])
    for cut in cuts[1:]:
        loudness = loudness * one(*cut)
    return loudness


def noise(own_key, extent, scale, most, shards=(), kind=jnp.bfloat16):
    level = block_levels(own_key, extent, shards, -0.22, 0.18) if shards else 1.0
    array = jax.random.normal(own_key, extent, jnp.float32) * scale * level
    return jnp.minimum(jnp.maximum(array, -most), most).astype(kind)


def setup_inputs(seed: int = 0, part: int = 0) -> dict:
    splits = jax.random.split(jax.random.key(seed), 4)
    part_keys = jax.random.split(jax.random.fold_in(splits[3], part), 4)
    return {
        "receptor": draw_receptor(jax.random.fold_in(splits[3], 71), part),
        "ligand_grids": noise(splits[1], (ROT_SET, CH, LB, LB * LB), 2.0, 8.0, ((2, 4),)),
        "rot_index": plant(jax.random.randint(part_keys[2], (ROTS,), 0, ROT_SET), jax.random.fold_in(part_keys[2], 1), 0, ROT_SET - 1).astype(jnp.int32),
    }


def reference(receptor, ligand_grids, rot_index):
    spectra = lax.complex(receptor[0].astype(jnp.float32), receptor[1].astype(jnp.float32))

    def one_rotation(which):
        grid = ligand_grids[which].astype(jnp.float32).reshape(CH, LB, LB, LB)
        padded = jnp.zeros((CH, N, N, N), jnp.float32).at[:, :LB, :LB, :LB].set(grid)
        ligand_spectrum = jnp.fft.fftn(padded, axes=(1, 2, 3))
        product = jnp.sum(spectra * jnp.conj(ligand_spectrum), axis=0)
        field = jnp.real(jnp.fft.ifftn(product))
        return jnp.transpose(field, (1, 2, 0))

    scores = lax.map(one_rotation, rot_index)
    best = jnp.min(scores, axis=(1, 2, 3))
    return scores, best
```

```python
import functools
import math

import jax
import jax.numpy as jnp
import ml_dtypes
import numpy as np
from jax import lax
from jax.experimental import pallas as pl
from jax.experimental.pallas import tpu as pltpu
from jax.sharding import PartitionSpec as P

STEP = 4
CHUNK = 2
BF = jnp.bfloat16
F32 = jnp.float32


def halves(table):
    upper = table.astype(np.float32).astype(ml_dtypes.bfloat16)
    lower = (table - upper.astype(np.float64)).astype(np.float32)
    return upper, lower.astype(ml_dtypes.bfloat16)


def trig(rows, cols, length):
    angle = (np.outer(rows, cols) % length) * (2.0 * math.pi / length)
    return np.cos(angle), np.sin(angle)


def split(values):
    upper = values.astype(BF)
    return upper, (values - upper.astype(F32)).astype(BF)


def mul(left, right):
    return jnp.dot(left, right, preferred_element_type=F32)


def mul_t(left, right):
    return lax.dot_general(left, right, (((1,), (1,)), ((), ())), preferred_element_type=F32)


def forward_kernel(channels, kept, half, a_ref, rec_ref, ty_ref, tx_ref, ti_ref, out_ref, b_re, b_im, p_re, p_im):
    per_group = 128 // 32
    for k in range(STEP):
        upper, lower = split(jnp.concatenate([a_ref[0, 0, k], a_ref[0, 1, k]], axis=0))
        both = mul(ty_ref[0], upper) + mul(ty_ref[0], lower) + mul(ty_ref[1], upper)
        b_re[k * kept : (k + 1) * kept, :] = both[:kept]
        b_im[k * kept : (k + 1) * kept, :] = both[kept:]
    for c in range(channels):
        lanes = slice((c // per_group) * 128, (c // per_group + 1) * 128)
        if c % per_group == 0:
            upper, lower = split(jnp.concatenate([b_re[:, lanes], b_im[:, lanes]], axis=1))
        t = c % per_group
        spec = mul(upper, tx_ref[0, t]) + mul(lower, tx_ref[0, t]) + mul(upper, tx_ref[1, t])
        s_re, s_im = spec[:, :128], spec[:, 128:]
        r_re = rec_ref[0, c].astype(F32).reshape(STEP * kept, 128)
        r_im = rec_ref[1, c].astype(F32).reshape(STEP * kept, 128)
        q_re = r_re * s_re + r_im * s_im
        q_im = r_im * s_re - r_re * s_im
        if c == 0:
            p_re[...] = q_re
            p_im[...] = q_im
        else:
            p_re[...] += q_re
            p_im[...] += q_im
    first = lax.broadcasted_iota(jnp.int32, (half, 128), 0) == 0
    for k in range(STEP):
        base = k * kept
        g_re = p_re[base : base + half, :]
        g_im = p_im[base : base + half, :]
        n_re = p_re[base + half : base + half + 1, :]
        n_im = p_im[base + half : base + half + 1, :]
        g_re, g_im = jnp.where(first, g_re - n_im, g_re), jnp.where(first, g_im + n_re, g_im)
        square = jnp.concatenate(
            [jnp.concatenate([g_re, 0.0 - g_im], axis=1), jnp.concatenate([g_im, g_re], axis=1)], axis=0
        )
        upper, lower = split(square)
        field = mul_t(ti_ref[0], upper) + mul_t(ti_ref[0], lower) + mul_t(ti_ref[1], upper)
        out_ref[0, :, k] = field.reshape(out_ref.shape[1], out_ref.shape[3], 128)


def final_kernel(groups, length, width, *refs):
    blocks, (tz_ref, tw_ref, out_ref, low_ref) = refs[:groups], refs[groups:]
    for i in range(width):
        upper, lower = split(jnp.concatenate([b[0, :, i, :] for b in blocks], axis=0))
        both = mul(tz_ref[0], upper) + mul(tz_ref[0], lower) + mul(tz_ref[1], upper)
        upper, lower = split(jnp.concatenate([both[:length], both[length:]], axis=1))
        plane = mul_t(tw_ref[0], upper) + mul_t(tw_ref[0], lower) + mul_t(tw_ref[1], upper)
        out_ref[0, i] = plane
        low_ref[0, i : i + 1, :] = jnp.min(plane, axis=0, keepdims=True)


def shards(receptor, ligand_grids, rot_index):
    groups = lax.axis_size("fft")
    me = lax.axis_index("fft")
    channels, slab, length = receptor.shape[1], receptor.shape[2], receptor.shape[3]
    box = ligand_grids.shape[2] * groups
    rotations = rot_index.shape[0]
    half = length // 2
    kept = half + 8
    xs = length // groups
    padded = -(-channels // 4) * 4
    freq, cells = np.arange(length), np.arange(box)

    def pair(table):
        return jnp.asarray(np.stack(halves(table)))

    def mine(tables):
        return lax.dynamic_index_in_dim(pair(np.stack(tables)), me, axis=1, keepdims=False)

    cos, sin = trig(freq, cells, length)
    t_z = mine([np.concatenate([cos[d * slab : (d + 1) * slab], -sin[d * slab : (d + 1) * slab]]) for d in range(groups)])
    cy, sy = cos[:kept], sin[:kept]
    t_y = pair(np.block([[cy, sy], [-sy, cy]]))
    tx = np.zeros((4, 256, 256))
    for t in range(4):
        tx[t, t * 32 : t * 32 + 32] = np.concatenate([cos.T, -sin.T], axis=1)
        tx[t, 128 + t * 32 : 128 + t * 32 + 32] = np.concatenate([sin.T, cos.T], axis=1)
    t_x = pair(tx)
    cf, sf = trig(freq, freq, length)
    whole = np.concatenate([cf, sf], axis=1)
    t_i = mine([np.roll(whole, -d * xs, axis=0) for d in range(groups)])
    def by_source(d):
        return np.concatenate([np.arange(slab) + ((d - s) % groups) * slab for s in range(groups)])

    both = np.concatenate([cf, sf], axis=0)
    t_b = mine([both[:, by_source(d)] for d in range(groups)])
    alpha, beta = 2.0 * cf[:, :half], -2.0 * sf[:, :half]
    alpha[:, 0], beta[:, 0] = 1.0, (-1.0) ** freq
    t_w = pair(np.concatenate([alpha, beta, beta, -alpha], axis=1) / float(length) ** 3)

    chosen = jnp.stack([lax.dynamic_index_in_dim(ligand_grids, rot_index[r], 0, keepdims=False) for r in range(rotations)])
    planes = lax.all_gather(chosen, "fft", axis=2, tiled=True)
    planes = planes.reshape(rotations, channels, box, box, box)
    planes = jnp.pad(planes, ((0, 0), (0, padded - channels), (0, 0), (0, 0), (0, 0)))
    planes = planes.transpose(0, 2, 4, 1, 3).reshape(rotations, box, box, padded * box)
    rec = receptor[..., :kept].transpose(0, 1, 2, 4, 3)

    def forward(part):
        count = part.shape[0]
        depth = jnp.einsum("kz,rzym->rkym", t_z[0], part, preferred_element_type=F32)
        depth = depth + jnp.einsum("kz,rzym->rkym", t_z[1], part, preferred_element_type=F32)
        depth = depth.reshape(count, 2, slab, box, padded * box)
        rows = STEP * kept
        return pl.pallas_call(
            functools.partial(forward_kernel, channels, kept, half),
            grid=(slab // STEP, count),
            in_specs=[
                pl.BlockSpec((1, 2, STEP, box, padded * box), lambda k, r: (r, 0, k, 0, 0)),
                pl.BlockSpec((2, channels, STEP, kept, length), lambda k, r: (0, 0, k, 0, 0)),
                pl.BlockSpec(t_y.shape, lambda k, r: (0, 0, 0)),
                pl.BlockSpec(t_x.shape, lambda k, r: (0, 0, 0, 0)),
                pl.BlockSpec(t_i.shape, lambda k, r: (0, 0, 0)),
            ],
            out_specs=pl.BlockSpec((1, groups, STEP, xs, length), lambda k, r: (r, 0, k, 0, 0)),
            out_shape=jax.ShapeDtypeStruct((count, groups, slab, xs, length), F32),
            scratch_shapes=[pltpu.VMEM((rows, padded * box), F32)] * 2 + [pltpu.VMEM((rows, length), F32)] * 2,
            compiler_params=pltpu.CompilerParams(vmem_limit_bytes=40 * 2**20),
            cost_estimate=pl.CostEstimate(flops=count * slab * 200_000_000, bytes_accessed=20_000_000, transcendentals=0),
        )(depth, rec, t_y, t_x, t_i)

    def exchange(field):
        out = [field[:, 0]]
        for s in range(1, groups):
            out.append(lax.ppermute(field[:, s], "fft", [(d, (d + s) % groups) for d in range(groups)]))
        return out

    width = 8

    def final(blocks):
        count = blocks[0].shape[0]
        return pl.pallas_call(
            functools.partial(final_kernel, groups, length, width),
            grid=(count, xs // width),
            in_specs=[pl.BlockSpec((1, slab, width, length), lambda r, x: (r, 0, x, 0))] * groups
            + [pl.BlockSpec(t_b.shape, lambda r, x: (0, 0, 0)), pl.BlockSpec(t_w.shape, lambda r, x: (0, 0, 0))],
            out_specs=[
                pl.BlockSpec((1, width, length, length), lambda r, x: (r, x, 0, 0)),
                pl.BlockSpec((1, width, length), lambda r, x: (r, x, 0)),
            ],
            out_shape=[
                jax.ShapeDtypeStruct((count, xs, length, length), F32),
                jax.ShapeDtypeStruct((count, xs, length), F32),
            ],
            compiler_params=pltpu.CompilerParams(vmem_limit_bytes=32 * 2**20),
            cost_estimate=pl.CostEstimate(flops=count * xs * 100_000_000, bytes_accessed=count * 4_000_000, transcendentals=0),
        )(*blocks, t_b, t_w)

    arrived = [exchange(forward(planes[r : r + CHUNK])) for r in range(0, rotations, CHUNK)]
    parts = [final(blocks) for blocks in arrived]
    scores = jnp.concatenate([p[0] for p in parts], axis=0)
    lows = jnp.concatenate([p[1] for p in parts], axis=0)
    best = lax.pmin(jnp.min(lows, axis=(1, 2)), "fft")
    return scores, best


def solution(mesh):
    placed = (P(None, None, "fft", None, None), P(None, None, "fft", None), P("rot"))
    return jax.shard_map(
        shards,
        mesh=mesh,
        in_specs=placed,
        out_specs=(P("rot", "fft", None, None), P("rot")),
        check_vma=False,
    )
```

```python
import functools
import math

import jax
import jax.numpy as jnp
import ml_dtypes
import numpy as np
from jax import lax
from jax.experimental import pallas as pl
from jax.experimental.pallas import tpu as pltpu
from jax.sharding import PartitionSpec as P

STEP = 4
CHUNK = 2
BF = jnp.bfloat16
F32 = jnp.float32


def halves(table):
    upper = table.astype(np.float32).astype(ml_dtypes.bfloat16)
    lower = (table - upper.astype(np.float64)).astype(np.float32)
    return upper, lower.astype(ml_dtypes.bfloat16)


def trig(rows, cols, length):
    angle = (np.outer(rows, cols) % length) * (2.0 * math.pi / length)
    return np.cos(angle), np.sin(angle)


def split(values):
    upper = values.astype(BF)
    return upper, (values - upper.astype(F32)).astype(BF)


def mul(left, right):
    return jnp.dot(left, right, preferred_element_type=F32)


def mul_t(left, right):
    return lax.dot_general(left, right, (((1,), (1,)), ((), ())), preferred_element_type=F32)


def forward_kernel(channels, kept, half, a_ref, rec_ref, ty_ref, tx_ref, ti_ref, out_ref, b_re, b_im, p_re, p_im):
    per_group = 128 // 32
    for k in range(STEP):
        upper, lower = split(jnp.concatenate([a_ref[0, 0, k], a_ref[0, 1, k]], axis=0))
        both = mul(ty_ref[0], upper) + mul(ty_ref[0], lower) + mul(ty_ref[1], upper)
        b_re[k * kept : (k + 1) * kept, :] = both[:kept]
        b_im[k * kept : (k + 1) * kept, :] = both[kept:]
    for c in range(channels):
        lanes = slice((c // per_group) * 128, (c // per_group + 1) * 128)
        if c % per_group == 0:
            upper, lower = split(jnp.concatenate([b_re[:, lanes], b_im[:, lanes]], axis=1))
        t = c % per_group
        spec = mul(upper, tx_ref[0, t]) + mul(lower, tx_ref[0, t]) + mul(upper, tx_ref[1, t])
        s_re, s_im = spec[:, :128], spec[:, 128:]
        r_re = rec_ref[0, c].astype(F32).reshape(STEP * kept, 128)
        r_im = rec_ref[1, c].astype(F32).reshape(STEP * kept, 128)
        q_re = r_re * s_re + r_im * s_im
        q_im = r_im * s_re - r_re * s_im
        if c == 0:
            p_re[...] = q_re
            p_im[...] = q_im
        else:
            p_re[...] += q_re
            p_im[...] += q_im
    first = lax.broadcasted_iota(jnp.int32, (half, 128), 0) == 0
    for k in range(STEP):
        base = k * kept
        g_re = p_re[base : base + half, :]
        g_im = p_im[base : base + half, :]
        n_re = p_re[base + half : base + half + 1, :]
        n_im = p_im[base + half : base + half + 1, :]
        g_re, g_im = jnp.where(first, g_re - n_im, g_re), jnp.where(first, g_im + n_re, g_im)
        square = jnp.concatenate(
            [jnp.concatenate([g_re, 0.0 - g_im], axis=1), jnp.concatenate([g_im, g_re], axis=1)], axis=0
        )
        upper, lower = split(square)
        field = mul_t(ti_ref[0], upper) + mul_t(ti_ref[0], lower) + mul_t(ti_ref[1], upper)
        out_ref[0, :, k] = field.reshape(out_ref.shape[1], out_ref.shape[3], 128)


def final_kernel(groups, length, width, *refs):
    blocks, tz_ref, tw_ref = refs[:groups], refs[groups], refs[groups + 1]
    out_ref, low_ref = refs[-2:]
    for i in range(width):
        upper, lower = split(jnp.concatenate([b[0, :, i, :] for b in blocks], axis=0))
        both = mul(tz_ref[0], upper) + mul(tz_ref[0], lower) + mul(tz_ref[1], upper)
        upper, lower = split(jnp.concatenate([both[:length], both[length:]], axis=1))
        plane = mul_t(tw_ref[0], upper) + mul_t(tw_ref[0], lower) + mul_t(tw_ref[1], upper)
        out_ref[0, i] = plane
        low_ref[0, i : i + 1, :] = jnp.min(plane, axis=0, keepdims=True)


def shards(receptor, ligand_grids, rot_index):
    groups = lax.axis_size("fft")
    me = lax.axis_index("fft")
    channels, slab, length = receptor.shape[1], receptor.shape[2], receptor.shape[3]
    box = ligand_grids.shape[2] * groups
    rotations = rot_index.shape[0]
    half = length // 2
    kept = half + 8
    xs = length // groups
    padded = -(-channels // 4) * 4
    freq, cells = np.arange(length), np.arange(box)

    def pair(table):
        return jnp.asarray(np.stack(halves(table)))

    def mine(tables):
        return lax.dynamic_index_in_dim(pair(np.stack(tables)), me, axis=1, keepdims=False)

    cos, sin = trig(freq, cells, length)
    t_z = mine([np.concatenate([cos[d * slab : (d + 1) * slab], -sin[d * slab : (d + 1) * slab]]) for d in range(groups)])
    cy, sy = cos[:kept], sin[:kept]
    t_y = pair(np.block([[cy, sy], [-sy, cy]]))
    tx = np.zeros((4, 256, 256))
    for t in range(4):
        tx[t, t * 32 : t * 32 + 32] = np.concatenate([cos.T, -sin.T], axis=1)
        tx[t, 128 + t * 32 : 128 + t * 32 + 32] = np.concatenate([sin.T, cos.T], axis=1)
    t_x = pair(tx)
    cf, sf = trig(freq, freq, length)
    whole = np.concatenate([cf, sf], axis=1)
    t_i = mine([np.roll(whole, -d * xs, axis=0) for d in range(groups)])
    def by_source(d):
        return np.concatenate([np.arange(slab) + ((d - s) % groups) * slab for s in range(groups)])

    both = np.concatenate([cf, sf], axis=0)
    t_b = mine([both[:, by_source(d)] for d in range(groups)])
    alpha, beta = 2.0 * cf[:, :half], -2.0 * sf[:, :half]
    alpha[:, 0], beta[:, 0] = 1.0, (-1.0) ** freq
    t_w = pair(np.concatenate([alpha, beta, beta, -alpha], axis=1) / float(length) ** 3)

    def gather(start):
        picks = range(start, start + CHUNK)
        own = jnp.stack([lax.dynamic_index_in_dim(ligand_grids, rot_index[r], 0, keepdims=False) for r in picks])
        own = own.reshape(CHUNK, channels, box // groups, box, box)
        own = jnp.pad(own, ((0, 0), (0, padded - channels), (0, 0), (0, 0), (0, 0)))
        own = own.transpose(0, 2, 4, 1, 3).reshape(CHUNK, box // groups, box, padded * box)
        return lax.all_gather(own, "fft", axis=1, tiled=True)

    rec = receptor[..., :kept].transpose(0, 1, 2, 4, 3)

    def forward(part):
        count = part.shape[0]
        depth = jnp.einsum("kz,rzym->rkym", t_z[0], part, preferred_element_type=F32)
        depth = depth + jnp.einsum("kz,rzym->rkym", t_z[1], part, preferred_element_type=F32)
        depth = depth.reshape(count, 2, slab, box, padded * box)
        rows = STEP * kept
        return pl.pallas_call(
            functools.partial(forward_kernel, channels, kept, half),
            grid=(slab // STEP, count),
            in_specs=[
                pl.BlockSpec((1, 2, STEP, box, padded * box), lambda k, r: (r, 0, k, 0, 0)),
                pl.BlockSpec((2, channels, STEP, kept, length), lambda k, r: (0, 0, k, 0, 0)),
                pl.BlockSpec(t_y.shape, lambda k, r: (0, 0, 0)),
                pl.BlockSpec(t_x.shape, lambda k, r: (0, 0, 0, 0)),
                pl.BlockSpec(t_i.shape, lambda k, r: (0, 0, 0)),
            ],
            out_specs=pl.BlockSpec((1, groups, STEP, xs, length), lambda k, r: (r, 0, k, 0, 0)),
            out_shape=jax.ShapeDtypeStruct((count, groups, slab, xs, length), F32),
            scratch_shapes=[pltpu.VMEM((rows, padded * box), F32)] * 2 + [pltpu.VMEM((rows, length), F32)] * 2,
            compiler_params=pltpu.CompilerParams(vmem_limit_bytes=40 * 2**20),
            cost_estimate=pl.CostEstimate(flops=count * slab * 200_000_000, bytes_accessed=20_000_000, transcendentals=0),
        )(depth, rec, t_y, t_x, t_i)

    def exchange(field):
        out = [field[:, 0]]
        for s in range(1, groups):
            out.append(lax.ppermute(field[:, s], "fft", [(d, (d + s) % groups) for d in range(groups)]))
        return out

    width = 8

    def final(start, blocks, before):
        count = blocks[0].shape[0]
        return pl.pallas_call(
            functools.partial(final_kernel, groups, length, width),
            grid=(count, xs // width),
            in_specs=[pl.BlockSpec((1, slab, width, length), lambda r, x: (r, 0, x, 0))] * groups
            + [pl.BlockSpec(t_b.shape, lambda r, x: (0, 0, 0)), pl.BlockSpec(t_w.shape, lambda r, x: (0, 0, 0))]
            + [pl.BlockSpec(memory_space=pl.ANY)] * len(before),
            out_specs=[
                pl.BlockSpec((1, width, length, length), lambda r, x: (start + r, x, 0, 0)),
                pl.BlockSpec((1, width, length), lambda r, x: (r, x, 0)),
            ],
            out_shape=[
                jax.ShapeDtypeStruct((rotations, xs, length, length), F32),
                jax.ShapeDtypeStruct((count, xs, length), F32),
            ],
            compiler_params=pltpu.CompilerParams(vmem_limit_bytes=32 * 2**20),
            cost_estimate=pl.CostEstimate(flops=count * xs * 100_000_000, bytes_accessed=count * 4_000_000, transcendentals=0),
            input_output_aliases={groups + 2: 0} if before else {},
        )(*blocks, t_b, t_w, *before)

    arrived = [exchange(forward(gather(r))) for r in range(0, rotations, CHUNK)]
    before, lows = (), []
    for index, blocks in enumerate(arrived):
        scores, low = final(index * CHUNK, blocks, before)
        before = (scores,)
        lows.append(low)
    lows = jnp.concatenate(lows, axis=0)
    best = lax.pmin(jnp.min(lows, axis=(1, 2)), "fft")
    return scores, best


def solution(mesh):
    placed = (P(None, None, "fft", None, None), P(None, None, "fft", None), P("rot"))
    return jax.shard_map(
        shards,
        mesh=mesh,
        in_specs=placed,
        out_specs=(P("rot", "fft", None, None), P("rot")),
        check_vma=False,
    )
```
